128 devices in a mesh: pb: 8 (over z_hi, x), ta: 16 (over z_lo, y, core).
Axes of the slice: x: 4, y: 4, z: 4 (z_hi: 2, z_lo: 2; z = z_hi * 2 + z_lo), core: 2. Of those that a mesh axis runs over, the one named last changes fastest.
Arguments:
- green: bfloat16 [8, 128, 256, 256], P(None, 'ta'), may hold values from -0.00059890747 to 0.00059890747
- colloc: bfloat16 [8, 384, 256], replicated, may hold values from -0.375 to 0.375
- kplus: int32 [8, 8], replicated, may hold values from 0 to 7, as said below
- to_freq: bfloat16 [128, 128], replicated, may hold values from -0.5 to 0.5
- to_time: bfloat16 [128, 128], replicated, may hold values from -0.5 to 0.5
- coulomb: bfloat16 [384, 384], replicated, may hold values from -438272 to 438272
Outputs:
- sigma: float32 [8, 128, 256, 256], P('pb', 'ta')
The draws below stay inside these ranges and needn't reach their ends.
Inputs may be any that keep to these rules, and one draw needn't show every extreme that they name: kplus is the addition table of a periodic mesh of 8 points numbered in some order: every row and every column is a permutation, and kplus[q, kplus[r, k]] = kplus[kplus[q, r], k]; row q is the transfer numbered q.
All inputs are finite; a program needn't handle non-finite values.
Results may differ from the reference program's by a relative error of at most 0.023.
Values may be sent and summed in bfloat16 or wider, within the bound.
A program may use at most 256 MiB of HBM per device.

```python
import jax
import jax.numpy as jnp
from jax import lax

NORB = 256
NAUX = 384
NTAU = 128
NK = 8


def draw_kplus(key, part):
    key = jax.random.fold_in(key, 7)
    labels = jax.random.permutation(key, NK).astype(jnp.int32)
    places = jnp.argsort(labels).astype(jnp.int32)
    summed = (places[:, None] + places[None, :]) % NK
    return labels[summed].astype(jnp.int32)


def block_scale(stream_key, extent, shards, least, top_value):
    factor_of, own = 1.0, jax.random.fold_in(stream_key, 6)
    for dim, blocks in shards:
        draws = jnp.exp(jax.random.uniform(jax.random.fold_in(own, dim), (blocks,), jnp.float32, least / len(shards), top_value / len(shards)))
        factor_of = factor_of * jnp.repeat(draws, extent[dim] // blocks).reshape([-1 if axis == dim else 1 for axis in range(len(extent))])
    return factor_of


def gaussian(stream_key, shape, scale, bound, cuts=(), kind=jnp.bfloat16):
    factor_of = block_scale(stream_key, shape, cuts, -0.22, 0.18) if cuts else 1.0
    array = jax.random.normal(stream_key, shape, jnp.float32) * scale * factor_of
    return jnp.minimum(jnp.maximum(array, -bound), bound).astype(kind)


def setup_inputs(seed: int = 0) -> dict:
    streams_of = jax.random.split(jax.random.key(seed), 7)
    green = gaussian(streams_of[0], (NK, NTAU, NORB, NORB), 0.0001, 0.00059890747, ((1, 16),))
    colloc = gaussian(streams_of[1], (NK, NAUX, NORB), NORB ** -0.5, 0.375)
    kplus = draw_kplus(jax.random.fold_in(streams_of[6], 71), 0)
    to_freq = gaussian(streams_of[3], (NTAU, NTAU), NTAU ** -0.5, 0.5)
    to_time = gaussian(streams_of[4], (NTAU, NTAU), NTAU ** -0.5, 0.5)
    coulomb = gaussian(streams_of[5], (NAUX, NAUX), 74000.0, 438272.0)
    return {"green": green, "colloc": colloc, "kplus": kplus, "to_freq": to_freq, "to_time": to_time, "coulomb": coulomb}


def project_point(pair):
    green_k, colloc_k = pair
    half_proj = jnp.einsum('tij,qj->tiq', green_k.astype(jnp.float32), colloc_k.astype(jnp.float32)).astype(jnp.bfloat16)
    return jnp.einsum('pi,tiq->tpq', colloc_k.astype(jnp.float32), half_proj.astype(jnp.float32)).astype(jnp.bfloat16)


def swap_pairs(values):
    shape = values.shape
    paired = values.reshape(shape[0], shape[1] // 2, 2, shape[2], shape[3])
    return paired[:, :, ::-1].reshape(shape)


def reference(green, colloc, kplus, to_freq, to_time, coulomb):
    aux_green = lax.map(project_point, (green, colloc))
    mirror = swap_pairs(aux_green)
    scale = -1.0 / NK
    coul = coulomb.astype(jnp.float32)
    point_ids = jnp.arange(NK).astype(jnp.int32)

    def per_transfer(total, plus_row):
        polar_sum = jnp.zeros((NTAU, NAUX, NAUX), jnp.float32)
        for point in range(NK):
            shifted = jnp.take(aux_green, plus_row[point], axis=0).astype(jnp.float32)
            polar_sum = polar_sum + shifted * jnp.swapaxes(mirror[point].astype(jnp.float32), 1, 2)
        polar = (scale * polar_sum).astype(jnp.bfloat16)
        freq_polar = jnp.einsum('wt,tpq->wpq', to_freq.astype(jnp.float32), polar.astype(jnp.float32)).astype(jnp.bfloat16)
        first = jnp.einsum('wpr,rq->wpq', freq_polar.astype(jnp.float32), coul).astype(jnp.bfloat16)
        series = (freq_polar.astype(jnp.float32) + jnp.einsum('wpr,wrq->wpq', first.astype(jnp.float32), freq_polar.astype(jnp.float32))).astype(jnp.bfloat16)
        left_prod = jnp.einsum('pr,wrq->wpq', coul, series.astype(jnp.float32)).astype(jnp.bfloat16)
        screen_freq = jnp.einsum('wpr,rq->wpq', left_prod.astype(jnp.float32), coul).astype(jnp.bfloat16)
        screen_time = jnp.einsum('tw,wpq->tpq', to_time.astype(jnp.float32), screen_freq.astype(jnp.float32)).astype(jnp.bfloat16)
        parts = []
        for target in range(NK):
            source = jnp.sum(jnp.where(plus_row == target, point_ids, 0)).astype(jnp.int32)
            hadamard = (jnp.take(aux_green, source, axis=0).astype(jnp.float32) * screen_time.astype(jnp.float32)).astype(jnp.bfloat16)
            own_colloc = colloc[target].astype(jnp.float32)
            right_prod = jnp.einsum('tpq,qj->tpj', hadamard.astype(jnp.float32), own_colloc)
            parts.append(jnp.einsum('pi,tpj->tij', own_colloc, right_prod, precision=lax.Precision.HIGHEST))
        return total + jnp.stack(parts), None

    start_total = jnp.zeros((NK, NTAU, NORB, NORB), jnp.float32)
    total, unused = lax.scan(per_transfer, start_total, kplus)
    return scale * total
```

```python
import jax
import jax.numpy as jnp
from jax import lax
from jax.experimental import pallas as pl
from jax.experimental.pallas import tpu as pltpu
from jax.sharding import PartitionSpec as P

MESH = pl.DeviceIdType.MESH
F32, BF16 = jnp.float32, jnp.bfloat16
NK = 8
NT = 8
GROUPS = 3
LANES = 128
MIB = 1 << 20


def dot(a, b, dims=((1,), (0,))):
    return lax.dot_general(a, b, (dims, ((), ())), preferred_element_type=F32)


def project_kernel(kplus_ref, green_ref, colloc_ref, aux_ref, polar_ref, aux_s, mirror_s):
    k = pl.program_id(0)
    p = lax.axis_index("pb")
    rows = jnp.concatenate(
        [colloc_ref[0, pl.ds(pl.multiple_of(128 * g + 16 * p, 16), 16), :] for g in range(GROUPS)], axis=0
    )
    colloc = colloc_ref[0]
    left, right = [], []
    for t in range(NT):
        left.append(dot(rows, green_ref[0, t]).astype(BF16))
        right.append(dot(rows, green_ref[0, t ^ 1], ((1,), (1,))).astype(BF16))
    aux = dot(jnp.concatenate(left, axis=0), colloc, ((1,), (1,))).astype(BF16)
    aux_ref[0] = aux.reshape(NT, 48, 384)
    aux_s[k] = aux.astype(F32).reshape(NT, 48, 384)
    mirror = dot(jnp.concatenate(right, axis=0), colloc, ((1,), (1,))).astype(BF16)
    mirror_s[k] = mirror.astype(F32).reshape(NT, 48, 384)

    @pl.when(k == NK - 1)
    def _():
        def step(i, carry):
            tp, q = i // NK, lax.rem(i, NK)
            for ch in range(GROUPS):
                cols = slice(LANES * ch, LANES * ch + LANES)
                total = None
                for point in range(NK):
                    term = aux_s[kplus_ref[q, point], pl.ds(2 * tp, 2), :, cols] * mirror_s[point, pl.ds(2 * tp, 2), :, cols]
                    total = term if total is None else total + term
                total = (total * (-1.0 / NK)).reshape(2, GROUPS, 2, 8, LANES)
                for g in range(GROUPS):
                    for core in range(2):
                        polar_ref[ch, 2 * q + core, pl.ds(pl.multiple_of(64 * g + 16 * tp, 16), 16), :] = (
                            total[:, g, core].reshape(16, LANES).astype(BF16)
                        )
            return carry

        lax.fori_loop(0, NK * NT // 2, step, 0)


def project(kplus, green, colloc):
    return pl.pallas_call(
        project_kernel,
        grid=(NK,),
        in_specs=[
            pl.BlockSpec(memory_space=pltpu.SMEM),
            pl.BlockSpec((1, NT, 256, 256), lambda k: (k, 0, 0, 0)),
            pl.BlockSpec((1, 384, 256), lambda k: (k, 0, 0)),
        ],
        out_specs=[
            pl.BlockSpec((1, NT, 48, 384), lambda k: (k, 0, 0, 0)),
            pl.BlockSpec((GROUPS, 16, 192, LANES), lambda k: (0, 0, 0, 0)),
        ],
        out_shape=[
            jax.ShapeDtypeStruct((NK, NT, 48, 384), BF16),
            jax.ShapeDtypeStruct((GROUPS, 16, 192, LANES), BF16),
        ],
        scratch_shapes=[pltpu.VMEM((NK, NT, 48, 384), F32), pltpu.VMEM((NK, NT, 48, 384), F32)],
        compiler_params=pltpu.CompilerParams(vmem_limit_bytes=48 * MIB),
        name="project",
    )(kplus, green, colloc)


def spread(table, wide_ref):
    row = lax.broadcasted_iota(jnp.int32, (1024, 128), 0) // 8
    pick = (row == lax.broadcasted_iota(jnp.int32, (1024, 128), 1)).astype(BF16)
    across = dot(table, pick, ((1,), (1,))).astype(BF16)
    for part in range(4):
        full = dot(pick[256 * part : 256 * part + 256], across)
        same = lax.broadcasted_iota(jnp.int32, (256, 1024), 0) % 8 == lax.broadcasted_iota(jnp.int32, (256, 1024), 1) % 8
        wide_ref[256 * part : 256 * part + 256, :] = jnp.where(same, full, 0.0).astype(BF16)


def transform(wide_ref, src, dst, ch):
    x = jnp.concatenate([src[ch, :, 64 * g : 64 * g + 64, :].reshape(1024, LANES) for g in range(GROUPS)], axis=1)
    for part in range(4):
        y = dot(wide_ref[256 * part : 256 * part + 256, :], x).astype(BF16)
        for g in range(GROUPS):
            dst[ch, 4 * part : 4 * part + 4, 64 * g : 64 * g + 64, :] = y[:, LANES * g : LANES * g + LANES].reshape(4, 64, LANES)


def screen_kernel(
    polar_ref, freq_ref, time_ref, coul_ref, out_ref,
    times, freqs, whole, chain, back, stamps, wide, send_sem, recv_sem, own_sem,
):
    pb, ta = lax.axis_index("pb"), lax.axis_index("ta")
    z_hi, z_lo, y, core = pb // 4, ta // 8, lax.rem(ta // 2, 4), lax.rem(ta, 2)
    own_q = y + 4 * lax.bitwise_xor(z_lo, z_hi)
    own_block = 2 * pb + core

    def line(j):
        return (pb, j)

    def plane(j):
        other = j // 2
        other_lo = lax.bitwise_xor(lax.bitwise_xor(z_lo, z_hi), other // 4)
        return (other, 8 * other_lo + 2 * y + lax.rem(j, 2))

    def transfer_slot(j):
        return 2 * (lax.rem(j // 2, 4) + 4 * lax.bitwise_xor(j // 8, z_hi)) + lax.rem(j, 2)

    same = lambda j: j
    stages = (
        (polar_ref, transfer_slot, times, ta, line, ta),
        (freqs, same, whole, own_block, plane, own_block),
        (chain, same, back, own_block, plane, own_block),
        (stamps, same, out_ref, 2 * own_q + core, line, ta),
    )

    def send(stage, ch):
        src, slot, dst, there, device, me = stages[stage]

        def go(s, carry):
            j = lax.bitwise_xor(me, s)
            pltpu.make_async_remote_copy(
                src_ref=src.at[ch, slot(j)],
                dst_ref=dst.at[ch, there],
                send_sem=send_sem.at[stage, ch],
                recv_sem=recv_sem.at[stage, ch],
                device_id=device(j),
                device_id_type=MESH,
            ).start()
            return carry

        lax.fori_loop(1, 16, go, 0)
        pltpu.make_async_copy(src.at[ch, slot(me)], dst.at[ch, there], own_sem.at[stage, ch]).start()

    def receive(stage, ch):
        src, slot, dst, there, device, me = stages[stage]
        part = dst.at[ch, pl.ds(0, 15)]
        pltpu.make_async_copy(part, part, recv_sem.at[stage, ch]).wait()
        pltpu.make_async_copy(src.at[ch, slot(me)], dst.at[ch, there], own_sem.at[stage, ch]).wait()

    def sent(stage, ch):
        part = stages[stage][0].at[ch, pl.ds(0, 15)]
        pltpu.make_async_copy(part, part, send_sem.at[stage, ch]).wait()

    barrier = pltpu.get_barrier_semaphore()

    def greet(s, carry):
        pl.semaphore_signal(barrier, inc=1, device_id=line(lax.bitwise_xor(ta, s)), device_id_type=MESH)
        pl.semaphore_signal(barrier, inc=1, device_id=plane(lax.bitwise_xor(own_block, s)), device_id_type=MESH)
        return carry

    lax.fori_loop(1, 16, greet, 0)
    pl.semaphore_wait(barrier, 30)

    send(0, 0)
    send(0, 1)
    spread(freq_ref[...], wide)
    for ch in range(GROUPS):
        receive(0, ch)
        if ch == 0:
            send(0, 2)
        transform(wide, times, freqs, ch)
        send(1, ch)
    spread(time_ref[...], wide)
    for ch in range(GROUPS):
        receive(1, ch)

    def pair(wp, carry):
        coul = coul_ref[...]
        lines = [
            [
                whole[ch, :, pl.ds(pl.multiple_of(64 * g + 16 * wp, 16), 16), :].astype(F32).reshape(16, 2, 8, LANES)
                for g in range(GROUPS)
            ]
            for ch in range(GROUPS)
        ]
        screened = []
        for j in range(2):
            polar = jnp.concatenate(
                [jnp.concatenate([lines[ch][g][:, j].reshape(128, LANES) for g in range(GROUPS)], axis=0) for ch in range(GROUPS)],
                axis=1,
            )
            low = polar.astype(BF16)
            first = dot(low, coul).astype(BF16)
            series = (polar + dot(first, low)).astype(BF16)
            left = dot(coul, series).astype(BF16)
            screened.append(dot(left, coul))
        for ch in range(GROUPS):
            for g in range(GROUPS):
                both = [
                    s[128 * g : 128 * g + 128, LANES * ch : LANES * ch + LANES].reshape(16, 1, 8, LANES) for s in screened
                ]
                chain[ch, :, pl.ds(pl.multiple_of(64 * g + 16 * wp, 16), 16), :] = (
                    jnp.concatenate(both, axis=1).reshape(16, 16, LANES).astype(BF16)
                )
        return carry

    lax.fori_loop(0, NT // 2, pair, 0)
    send(2, 0)
    send(2, 1)
    for ch in range(GROUPS):
        receive(2, ch)
        if ch == 0:
            send(2, 2)
        transform(wide, back, stamps, ch)
        send(3, ch)
    for ch in range(GROUPS):
        receive(3, ch)
    for stage in range(4):
        for ch in range(GROUPS):
            sent(stage, ch)


def screen(polar, to_freq, to_time, coulomb):
    block = (GROUPS, 16, 192, LANES)
    vmem = pl.BlockSpec(memory_space=pltpu.VMEM)
    hbm = pl.BlockSpec(memory_space=pl.ANY)
    return pl.pallas_call(
        screen_kernel,
        in_specs=[hbm, vmem, vmem, vmem],
        out_specs=hbm,
        out_shape=jax.ShapeDtypeStruct(block, BF16),
        scratch_shapes=[pltpu.VMEM(block, BF16)] * 6
        + [pltpu.VMEM((1024, 1024), BF16)]
        + [pltpu.SemaphoreType.DMA((4, GROUPS))] * 3,
        compiler_params=pltpu.CompilerParams(collective_id=0, has_side_effects=True, vmem_limit_bytes=48 * MIB),
        name="screen",
    )(polar, to_freq, to_time, coulomb)


def hadamard_kernel(source_ref, aux_ref, screen_ref, colloc_ref, out_ref, screen_s, sum_s):
    def step(tp, carry):
        for q in range(NK):
            for ch in range(GROUPS):
                for g in range(GROUPS):
                    for core in range(2):
                        part = screen_ref[ch, 2 * q + core, pl.ds(pl.multiple_of(64 * g + 16 * tp, 16), 16), :].astype(F32)
                        screen_s[q, :, 16 * g + 8 * core : 16 * g + 8 * core + 8, LANES * ch : LANES * ch + LANES] = (
                            part.reshape(2, 8, LANES)
                        )

        def target(c, inner):
            for ch in range(GROUPS):
                cols = slice(LANES * ch, LANES * ch + LANES)
                total = None
                for q in range(NK):
                    term = aux_ref[source_ref[q, c], pl.ds(2 * tp, 2), :, cols].astype(F32) * screen_s[q, :, :, cols]
                    total = term if total is None else total + term
                sum_s[c, pl.ds(pl.multiple_of(96 * tp, 32), 96), cols] = total.astype(BF16).reshape(96, LANES)
            return inner

        lax.fori_loop(0, NK, target, 0)
        return carry

    lax.fori_loop(0, NT // 2, step, 0)

    def project_out(c, carry):
        out_ref[c] = dot(sum_s[c], colloc_ref[c]).astype(BF16).reshape(NT, GROUPS, 16, 256)
        return carry

    lax.fori_loop(0, NK, project_out, 0)


def hadamard(sources, aux, screened, colloc):
    vmem = pl.BlockSpec(memory_space=pltpu.VMEM)
    return pl.pallas_call(
        hadamard_kernel,
        in_specs=[pl.BlockSpec(memory_space=pltpu.SMEM), vmem, vmem, vmem],
        out_specs=vmem,
        out_shape=jax.ShapeDtypeStruct((NK, NT, GROUPS, 16, 256), BF16),
        scratch_shapes=[pltpu.VMEM((NK, 2, 48, 384), F32), pltpu.VMEM((NK, NT * 48, 384), BF16)],
        compiler_params=pltpu.CompilerParams(vmem_limit_bytes=48 * MIB),
        name="hadamard",
    )(sources, aux, screened, colloc)


def exchange_kernel(src, dst, send_sem, recv_sem, own_sem):
    pb, ta = lax.axis_index("pb"), lax.axis_index("ta")
    barrier = pltpu.get_barrier_semaphore()

    def greet(s, carry):
        pl.semaphore_signal(barrier, inc=1, device_id=(lax.bitwise_xor(pb, s), ta), device_id_type=MESH)
        return carry

    lax.fori_loop(1, NK, greet, 0)
    pl.semaphore_wait(barrier, NK - 1)

    def go(s, carry):
        j = lax.bitwise_xor(pb, s)
        pltpu.make_async_remote_copy(
            src_ref=src.at[j],
            dst_ref=dst.at[pb],
            send_sem=send_sem,
            recv_sem=recv_sem,
            device_id=(j, ta),
            device_id_type=MESH,
        ).start()
        return carry

    lax.fori_loop(1, NK, go, 0)
    own = pltpu.make_async_copy(src.at[pb], dst.at[pb], own_sem)
    own.start()
    own.wait()
    part = dst.at[pl.ds(0, NK - 1)]
    pltpu.make_async_copy(part, part, send_sem).wait()
    pltpu.make_async_copy(part, part, recv_sem).wait()


def exchange(right):
    hbm = pl.BlockSpec(memory_space=pl.ANY)
    return pl.pallas_call(
        exchange_kernel,
        in_specs=[hbm],
        out_specs=hbm,
        out_shape=jax.ShapeDtypeStruct(right.shape, BF16),
        scratch_shapes=[pltpu.SemaphoreType.DMA] * 3,
        compiler_params=pltpu.CompilerParams(collective_id=1, has_side_effects=True),
        name="exchange",
    )(right)


def sigma_kernel(place_ref, right_ref, colloc_ref, out_ref):
    right = right_ref[...].reshape(NK, GROUPS, 16, 256)
    whole = jnp.concatenate([right[:, g].reshape(128, 256) for g in range(GROUPS)], axis=0)
    out_ref[0, 0] = dot(colloc_ref[0], whole, ((0,), (0,))) * (-1.0 / NK)


def outer(right, colloc, place):
    return pl.pallas_call(
        sigma_kernel,
        grid_spec=pltpu.PrefetchScalarGridSpec(
            num_scalar_prefetch=1,
            grid=(NT,),
            in_specs=[
                pl.BlockSpec((NK, 1, GROUPS, 16, 256), lambda t, place: (0, t, 0, 0, 0)),
                pl.BlockSpec((1, 384, 256), lambda t, place: (place[0], 0, 0)),
            ],
            out_specs=pl.BlockSpec((1, 1, 256, 256), lambda t, place: (0, t, 0, 0)),
        ),
        out_shape=jax.ShapeDtypeStruct((1, NT, 256, 256), F32),
        name="sigma",
    )(place, right, colloc)


def local(green, colloc, kplus, to_freq, to_time, coulomb):
    points = jnp.arange(NK, dtype=jnp.int32)
    sources = jnp.sum(jnp.where(kplus[:, :, None] == points[None, None, :], points[None, :, None], 0), axis=1)
    aux, polar = project(kplus, green, colloc)
    screened = screen(polar, to_freq, to_time, coulomb)
    right = exchange(hadamard(sources, aux, screened, colloc))
    return outer(right, colloc, lax.axis_index("pb").astype(jnp.int32).reshape(1))


def solution(mesh):
    in_specs = (P(None, "ta", None, None), P(), P(), P(), P(), P())
    out_specs = P("pb", "ta", None, None)
    return jax.shard_map(local, mesh=mesh, in_specs=in_specs, out_specs=out_specs, check_vma=False)
```

```python
import jax
import jax.numpy as jnp
from jax import lax
from jax.experimental import pallas as pl
from jax.experimental.pallas import tpu as pltpu
from jax.sharding import PartitionSpec as P

MESH = pl.DeviceIdType.MESH
F32, BF16 = jnp.float32, jnp.bfloat16
NK = 8
NT = 8
GROUPS = 3
PARTS = GROUPS * GROUPS
LANES = 128
MIB = 1 << 20


def dot(a, b, dims=((1,), (0,))):
    return lax.dot_general(a, b, (dims, ((), ())), preferred_element_type=F32)


def spread(table, wide_ref):
    row = lax.broadcasted_iota(jnp.int32, (1024, 128), 0) // 8
    pick = (row == lax.broadcasted_iota(jnp.int32, (1024, 128), 1)).astype(BF16)
    across = dot(table, pick, ((1,), (1,))).astype(BF16)
    for part in range(4):
        full = dot(pick[256 * part : 256 * part + 256], across)
        same = lax.broadcasted_iota(jnp.int32, (256, 1024), 0) % 8 == lax.broadcasted_iota(jnp.int32, (256, 1024), 1) % 8
        wide_ref[256 * part : 256 * part + 256, :] = jnp.where(same, full, 0.0).astype(BF16)


def transform(wide_ref, src, dst, n):
    x = src[n].reshape(1024, LANES)
    for part in range(4):
        y = dot(wide_ref[256 * part : 256 * part + 256, :], x)
        dst[n, 4 * part : 4 * part + 4] = y.astype(BF16).reshape(4, 64, LANES)


def step_kernel(
    kplus_ref, source_ref, green_ref, colloc_ref, freq_ref, time_ref, coul_ref, out_ref,
    green_s, colloc_s, left_s, right_s, aux_s, mirror_s, polar, times, freqs, whole, chain, back, stamps, screen, wide,
    sum_s, half_s, load_sem, send_sem, recv_sem, own_sem, last_send, last_recv, last_own,
):
    pb, ta = lax.axis_index("pb"), lax.axis_index("ta")
    z_hi, z_lo, y, core = pb // 4, ta // 8, lax.rem(ta // 2, 4), lax.rem(ta, 2)
    own_q = y + 4 * lax.bitwise_xor(z_lo, z_hi)
    own_block = 2 * pb + core

    def load(k):
        return pltpu.make_async_copy(green_ref.at[k], green_s.at[k], load_sem.at[k])

    load_colloc = pltpu.make_async_copy(colloc_ref, colloc_s, load_sem.at[NK])
    load_colloc.start()
    for k in range(NK):
        load(k).start()

    def line(j):
        return (pb, j)

    def plane(j):
        other = j // 2
        other_lo = lax.bitwise_xor(lax.bitwise_xor(z_lo, z_hi), other // 4)
        return (other, 8 * other_lo + 2 * y + lax.rem(j, 2))

    def transfer_slot(j):
        return 2 * (lax.rem(j // 2, 4) + 4 * lax.bitwise_xor(j // 8, z_hi)) + lax.rem(j, 2)

    same = lambda j: j
    stages = (
        (polar, transfer_slot, times, ta, line, ta),
        (freqs, same, whole, own_block, plane, own_block),
        (chain, same, back, own_block, plane, own_block),
        (stamps, same, screen, 2 * own_q + core, line, ta),
    )

    def send(stage, n, first=0, size=64):
        src, slot, dst, there, device, me = stages[stage]
        rows = pl.ds(first, size)

        def go(s, carry):
            j = lax.bitwise_xor(me, s)
            pltpu.make_async_remote_copy(
                src_ref=src.at[n, slot(j), rows],
                dst_ref=dst.at[n, there, rows],
                send_sem=send_sem.at[stage, n],
                recv_sem=recv_sem.at[stage, n],
                device_id=device(j),
                device_id_type=MESH,
            ).start()
            return carry

        lax.fori_loop(1, 16, go, 0)
        pltpu.make_async_copy(src.at[n, slot(me), rows], dst.at[n, there, rows], own_sem.at[stage, n]).start()

    def receive(stage, n):
        src, slot, dst, there, device, me = stages[stage]
        part = dst.at[n, pl.ds(0, 15)]
        pltpu.make_async_copy(part, part, recv_sem.at[stage, n]).wait()
        pltpu.make_async_copy(src.at[n, slot(me)], dst.at[n, there], own_sem.at[stage, n]).wait()

    def sent(stage, n):
        part = stages[stage][0].at[n, pl.ds(0, 15)]
        pltpu.make_async_copy(part, part, send_sem.at[stage, n]).wait()

    barrier = pltpu.get_barrier_semaphore()

    def greet(s, carry):
        pl.semaphore_signal(barrier, inc=1, device_id=line(lax.bitwise_xor(ta, s)), device_id_type=MESH)
        pl.semaphore_signal(barrier, inc=1, device_id=plane(lax.bitwise_xor(own_block, s)), device_id_type=MESH)
        return carry

    def greet_last(s, carry):
        pl.semaphore_signal(barrier, inc=1, device_id=(lax.bitwise_xor(pb, s), ta), device_id_type=MESH)
        return carry

    lax.fori_loop(1, 16, greet, 0)
    lax.fori_loop(1, NK, greet_last, 0)

    load_colloc.wait()

    def project(k, carry):
        load(k).wait()
        rows = jnp.concatenate(
            [colloc_s[k, pl.ds(pl.multiple_of(128 * g + 16 * pb, 16), 16), :] for g in range(GROUPS)], axis=0
        )
        left = [dot(rows, green_s[k, t]).reshape(6, 1, 8, 256) for t in range(NT)]
        right = [dot(rows, green_s[k, t ^ 1], ((1,), (1,))).reshape(6, 1, 8, 256) for t in range(NT)]
        left_s[k] = jnp.concatenate(left, axis=1).reshape(384, 256).astype(BF16)
        right_s[k] = jnp.concatenate(right, axis=1).reshape(384, 256).astype(BF16)
        return carry

    lax.fori_loop(0, NK, project, 0)
    pl.semaphore_wait(barrier, 30 + NK - 1)

    for ch in range(GROUPS):

        def widen(k, carry):
            columns = colloc_s[k, LANES * ch : LANES * ch + LANES, :]
            aux = dot(left_s[k], columns, ((1,), (1,)))
            mirror = dot(right_s[k], columns, ((1,), (1,)))
            for g in range(GROUPS):
                aux_s[3 * ch + g, k] = aux[128 * g : 128 * g + 128]
                mirror_s[g, k] = mirror[128 * g : 128 * g + 128]
            return carry

        lax.fori_loop(0, NK, widen, 0)
        for g in range(GROUPS):
            n = 3 * ch + g

            def polarize(i, carry):
                rows = pl.ds(pl.multiple_of(32 * i, 32), 32)
                mirrors = [mirror_s[g, k, rows, :] for k in range(NK)]
                for q in range(NK):
                    total = None
                    for k in range(NK):
                        term = aux_s[n, kplus_ref[q, k], rows, :] * mirrors[k]
                        total = term if total is None else total + term
                    polar[n, 2 * q + i // 2, pl.ds(pl.multiple_of(32 * lax.rem(i, 2), 32), 32), :] = (
                        total * (-1.0 / NK)
                    ).astype(BF16)
                return carry

            lax.fori_loop(0, 4, polarize, 0)
            send(0, n)

    spread(freq_ref[...], wide)
    for n in range(PARTS):
        receive(0, n)
        transform(wide, times, freqs, n)
        send(1, n)
    spread(time_ref[...], wide)
    for n in range(PARTS):
        receive(1, n)

    def pair(wp, carry):
        coul = coul_ref[...]
        rows = pl.ds(pl.multiple_of(16 * wp, 16), 16)
        lines = [whole[n, :, rows, :].astype(F32).reshape(16, 2, 8, LANES) for n in range(PARTS)]
        screened = []
        for j in range(2):
            full = jnp.concatenate(
                [
                    jnp.concatenate([lines[3 * ch + g][:, j].reshape(128, LANES) for g in range(GROUPS)], axis=0)
                    for ch in range(GROUPS)
                ],
                axis=1,
            )
            low = full.astype(BF16)
            first = dot(low, coul).astype(BF16)
            series = (full + dot(first, low)).astype(BF16)
            left = dot(coul, series).astype(BF16)
            screened.append(dot(left, coul))
        for ch in range(GROUPS):
            for g in range(GROUPS):
                both = [
                    s[128 * g : 128 * g + 128, LANES * ch : LANES * ch + LANES].reshape(16, 1, 8, LANES) for s in screened
                ]
                chain[3 * ch + g, :, rows, :] = jnp.concatenate(both, axis=1).reshape(16, 16, LANES).astype(BF16)
        return carry

    order = [3 * ch + g for g in range(GROUPS) for ch in range(GROUPS)]
    ahead = 3
    lax.fori_loop(0, 2, pair, 0)
    for n in order[:ahead]:
        send(2, n, 0, 32)
    lax.fori_loop(2, 4, pair, 0)
    for at, n in enumerate(order):
        send(2, n, 32, 32)
        if at + ahead < PARTS:
            send(2, order[at + ahead], 0, 32)

    last = []
    for at, n in enumerate(order):
        receive(2, n)
        transform(wide, back, stamps, n)
        send(3, n)
    for g in range(GROUPS):
        for ch in range(GROUPS):
            n = 3 * ch + g
            receive(3, n)

            def weigh(i, carry):
                rows = pl.ds(pl.multiple_of(32 * i, 32), 32)
                here = pl.ds(pl.multiple_of(32 * lax.rem(i, 2), 32), 32)
                screens = [screen[n, 2 * q + i // 2, here, :].astype(F32) for q in range(NK)]
                for c in range(NK):
                    total = None
                    for q in range(NK):
                        term = aux_s[n, source_ref[q, c], rows, :] * screens[q]
                        total = term if total is None else total + term
                    sum_s[c, rows, LANES * ch : LANES * ch + LANES] = total.astype(BF16)
                return carry

            lax.fori_loop(0, 4, weigh, 0)

        def halve(s, carry):
            c = lax.bitwise_xor(pb, s)
            half_s[g, c] = dot(sum_s[c], colloc_s[c]).astype(BF16)

            @pl.when(s > 0)
            def _():
                pltpu.make_async_remote_copy(
                    src_ref=half_s.at[g, c],
                    dst_ref=out_ref.at[g, pb],
                    send_sem=last_send.at[g],
                    recv_sem=last_recv.at[g],
                    device_id=(c, ta),
                    device_id_type=MESH,
                ).start()

            return carry

        lax.fori_loop(0, NK, halve, 0)
        own = pltpu.make_async_copy(half_s.at[g, pb], out_ref.at[g, pb], last_own.at[g])
        own.start()
        last.append(own)
    for g in range(GROUPS):
        last[g].wait()
        part = out_ref.at[g, pl.ds(0, NK - 1)]
        pltpu.make_async_copy(part, part, last_recv.at[g]).wait()
        part = half_s.at[g, pl.ds(0, NK - 1)]
        pltpu.make_async_copy(part, part, last_send.at[g]).wait()
    for stage in range(4):
        for n in range(PARTS):
            sent(stage, n)


def step(kplus, sources, green, colloc, to_freq, to_time, coulomb):
    block = (PARTS, 16, 64, LANES)
    vmem = pl.BlockSpec(memory_space=pltpu.VMEM)
    smem = pl.BlockSpec(memory_space=pltpu.SMEM)
    hbm = pl.BlockSpec(memory_space=pl.ANY)
    dma = pltpu.SemaphoreType.DMA
    return pl.pallas_call(
        step_kernel,
        in_specs=[smem, smem, hbm, hbm, vmem, vmem, vmem],
        out_specs=hbm,
        out_shape=jax.ShapeDtypeStruct((GROUPS, NK, 128, 256), BF16),
        scratch_shapes=[
            pltpu.VMEM((NK, NT, 256, 256), BF16),
            pltpu.VMEM((NK, 384, 256), BF16),
            pltpu.VMEM((NK, 384, 256), BF16),
            pltpu.VMEM((NK, 384, 256), BF16),
            pltpu.VMEM((PARTS, NK, 128, LANES), F32),
            pltpu.VMEM((GROUPS, NK, 128, LANES), F32),
        ]
        + [pltpu.VMEM(block, BF16)] * 8
        + [
            pltpu.VMEM((1024, 1024), BF16),
            pltpu.VMEM((NK, 128, 384), BF16),
            pltpu.VMEM((GROUPS, NK, 128, 256), BF16),
            dma((NK + 1,)),
            dma((4, PARTS)),
            dma((4, PARTS)),
            dma((4, PARTS)),
            dma((GROUPS,)),
            dma((GROUPS,)),
            dma((GROUPS,)),
        ],
        compiler_params=pltpu.CompilerParams(collective_id=0, has_side_effects=True, vmem_limit_bytes=56 * MIB),
        name="step",
    )(kplus, sources, green, colloc, to_freq, to_time, coulomb)


def sigma_kernel(place_ref, half_ref, colloc_ref, out_ref):
    half = half_ref[...].astype(F32).reshape(GROUPS, NK, 2, 2, 8, 256)
    for j in range(2):
        whole = half[:, :, :, j].reshape(384, 256).astype(BF16)
        out_ref[0, j] = dot(colloc_ref[0], whole, ((0,), (0,))) * (-1.0 / NK)


def sigma(half, colloc, place):
    return pl.pallas_call(
        sigma_kernel,
        grid_spec=pltpu.PrefetchScalarGridSpec(
            num_scalar_prefetch=1,
            grid=(NT // 2,),
            in_specs=[
                pl.BlockSpec((GROUPS, NK, 2, 16, 256), lambda tp, place: (0, 0, 0, tp, 0)),
                pl.BlockSpec((1, 384, 256), lambda tp, place: (place[0], 0, 0)),
            ],
            out_specs=pl.BlockSpec((1, 2, 256, 256), lambda tp, place: (0, tp, 0, 0)),
        ),
        out_shape=jax.ShapeDtypeStruct((1, NT, 256, 256), F32),
        name="sigma",
    )(place, half.reshape(GROUPS, NK, 2, 64, 256), colloc)


def local(green, colloc, kplus, to_freq, to_time, coulomb):
    points = jnp.arange(NK, dtype=jnp.int32)
    sources = jnp.sum(jnp.where(kplus[:, :, None] == points[None, None, :], points[None, :, None], 0), axis=1)
    half = step(kplus, sources, green, colloc, to_freq, to_time, coulomb)
    return sigma(half, colloc, lax.axis_index("pb").astype(jnp.int32).reshape(1))


def solution(mesh):
    in_specs = (P(None, "ta", None, None), P(), P(), P(), P(), P())
    out_specs = P("pb", "ta", None, None)
    return jax.shard_map(local, mesh=mesh, in_specs=in_specs, out_specs=out_specs, check_vma=False)
```

```python
import jax
import jax.numpy as jnp
from jax import lax
from jax.experimental import pallas as pl
from jax.experimental.pallas import tpu as pltpu
from jax.sharding import PartitionSpec as P

MESH = pl.DeviceIdType.MESH
F32, BF16 = jnp.float32, jnp.bfloat16
NK = 8
NT = 8
GROUPS = 3
PARTS = GROUPS * GROUPS
LANES = 128
MIB = 1 << 20


def dot(a, b, dims=((1,), (0,))):
    return lax.dot_general(a, b, (dims, ((), ())), preferred_element_type=F32)


def spread(table, wide_ref):
    row = lax.broadcasted_iota(jnp.int32, (1024, 128), 0) // 8
    pick = (row == lax.broadcasted_iota(jnp.int32, (1024, 128), 1)).astype(BF16)
    across = dot(table, pick, ((1,), (1,))).astype(BF16)
    for part in range(4):
        full = dot(pick[256 * part : 256 * part + 256], across)
        same = lax.broadcasted_iota(jnp.int32, (256, 1024), 0) % 8 == lax.broadcasted_iota(jnp.int32, (256, 1024), 1) % 8
        wide_ref[256 * part : 256 * part + 256, :] = jnp.where(same, full, 0.0).astype(BF16)


def transform(wide_ref, src, dst, n):
    x = src[n].reshape(1024, LANES)
    for part in range(4):
        y = dot(wide_ref[256 * part : 256 * part + 256, :], x)
        dst[n, 4 * part : 4 * part + 4] = y.astype(BF16).reshape(4, 64, LANES)


def step_kernel(
    kplus_ref, green_ref, colloc_ref, freq_ref, time_ref, coul_ref, out_ref,
    green_s, colloc_s, left_s, right_s, aux_s, mirror_s, polar, times, freqs, whole, chain, back, stamps, screen, wide,
    late_wide, sum_s, half_s, source_ref, load_sem, send_sem, recv_sem, own_sem, last_send, last_recv, last_own,
):
    pb, ta = lax.axis_index("pb"), lax.axis_index("ta")
    z_hi, z_lo, y, core = pb // 4, ta // 8, lax.rem(ta // 2, 4), lax.rem(ta, 2)
    own_q = y + 4 * lax.bitwise_xor(z_lo, z_hi)
    own_block = 2 * pb + core

    def load(k):
        return pltpu.make_async_copy(green_ref.at[k], green_s.at[k], load_sem.at[k])

    load_colloc = pltpu.make_async_copy(colloc_ref, colloc_s, load_sem.at[NK])
    load_colloc.start()
    for k in range(NK):
        load(k).start()

    def line(j):
        return (pb, j)

    def plane(j):
        other = j // 2
        other_lo = lax.bitwise_xor(lax.bitwise_xor(z_lo, z_hi), other // 4)
        return (other, 8 * other_lo + 2 * y + lax.rem(j, 2))

    def transfer_slot(j):
        return 2 * (lax.rem(j // 2, 4) + 4 * lax.bitwise_xor(j // 8, z_hi)) + lax.rem(j, 2)

    same = lambda j: j
    stages = (
        (polar, transfer_slot, times, ta, line, ta),
        (freqs, same, whole, own_block, plane, own_block),
        (chain, same, back, own_block, plane, own_block),
        (stamps, same, screen, 2 * own_q + core, line, ta),
    )

    def send(stage, n, first=0, size=64):
        src, slot, dst, there, device, me = stages[stage]
        rows = pl.ds(first, size)

        def go(s, carry):
            j = lax.bitwise_xor(me, s)
            pltpu.make_async_remote_copy(
                src_ref=src.at[n, slot(j), rows],
                dst_ref=dst.at[n, there, rows],
                send_sem=send_sem.at[stage, n],
                recv_sem=recv_sem.at[stage, n],
                device_id=device(j),
                device_id_type=MESH,
            ).start()
            return carry

        lax.fori_loop(1, 16, go, 0)
        pltpu.make_async_copy(src.at[n, slot(me), rows], dst.at[n, there, rows], own_sem.at[stage, n]).start()

    def receive(stage, n):
        src, slot, dst, there, device, me = stages[stage]
        part = dst.at[n, pl.ds(0, 15)]
        pltpu.make_async_copy(part, part, recv_sem.at[stage, n]).wait()
        pltpu.make_async_copy(src.at[n, slot(me)], dst.at[n, there], own_sem.at[stage, n]).wait()

    def sent(stage, n):
        part = stages[stage][0].at[n, pl.ds(0, 15)]
        pltpu.make_async_copy(part, part, send_sem.at[stage, n]).wait()

    barrier = pltpu.get_barrier_semaphore()

    def greet(s, carry):
        pl.semaphore_signal(barrier, inc=1, device_id=line(lax.bitwise_xor(ta, s)), device_id_type=MESH)
        pl.semaphore_signal(barrier, inc=1, device_id=plane(lax.bitwise_xor(own_block, s)), device_id_type=MESH)
        return carry

    def greet_last(s, carry):
        pl.semaphore_signal(barrier, inc=1, device_id=(lax.bitwise_xor(pb, s), ta), device_id_type=MESH)
        return carry

    lax.fori_loop(1, 16, greet, 0)
    lax.fori_loop(1, NK, greet_last, 0)

    load_colloc.wait()

    def project(k, carry):
        load(k).wait()
        rows = jnp.concatenate(
            [colloc_s[k, pl.ds(pl.multiple_of(128 * g + 16 * pb, 16), 16), :] for g in range(GROUPS)], axis=0
        )
        left = [dot(rows, green_s[k, t]).reshape(6, 1, 8, 256) for t in range(NT)]
        right = [dot(rows, green_s[k, t ^ 1], ((1,), (1,))).reshape(6, 1, 8, 256) for t in range(NT)]
        left_s[k] = jnp.concatenate(left, axis=1).reshape(384, 256).astype(BF16)
        right_s[k] = jnp.concatenate(right, axis=1).reshape(384, 256).astype(BF16)
        return carry

    lax.fori_loop(0, NK, project, 0)
    pl.semaphore_wait(barrier, 30 + NK - 1)

    for ch in range(GROUPS):

        def widen(k, carry):
            columns = colloc_s[k, LANES * ch : LANES * ch + LANES, :]
            aux = dot(left_s[k], columns, ((1,), (1,)))
            mirror = dot(right_s[k], columns, ((1,), (1,)))
            for g in range(GROUPS):
                aux_s[3 * ch + g, k] = aux[128 * g : 128 * g + 128]
                mirror_s[g, k] = mirror[128 * g : 128 * g + 128]
            return carry

        lax.fori_loop(0, NK, widen, 0, unroll=True)
        for g in range(GROUPS):
            n = 3 * ch + g

            def polarize(i, carry):
                rows = pl.ds(pl.multiple_of(32 * i, 32), 32)
                mirrors = [mirror_s[g, k, rows, :] for k in range(NK)]
                for q in range(NK):
                    total = None
                    for k in range(NK):
                        term = aux_s[n, kplus_ref[q, k], rows, :] * mirrors[k]
                        total = term if total is None else total + term
                    polar[n, 2 * q + i // 2, pl.ds(pl.multiple_of(32 * lax.rem(i, 2), 32), 32), :] = (
                        total * (-1.0 / NK)
                    ).astype(BF16)
                return carry

            lax.fori_loop(0, 4, polarize, 0)
            send(0, n)
        if ch == 0:
            spread(freq_ref[...], wide)

    def find(i, carry):
        q, c = i // NK, lax.rem(i, NK)
        found = jnp.int32(0)
        for k in range(NK):
            found = jnp.where(kplus_ref[q, k] == c, k, found)
        source_ref[q, c] = found
        return carry

    for n in range(PARTS):
        receive(0, n)
        transform(wide, times, freqs, n)
        send(1, n)
        if n == PARTS // 2:
            spread(time_ref[...], late_wide)
            lax.fori_loop(0, NK * NK, find, 0)
    for n in range(PARTS):
        receive(1, n)

    def pair(wp, carry):
        coul = coul_ref[...]
        rows = pl.ds(pl.multiple_of(16 * wp, 16), 16)
        lines = [whole[n, :, rows, :].astype(F32).reshape(16, 2, 8, LANES) for n in range(PARTS)]
        screened = []
        for j in range(2):
            full = jnp.concatenate(
                [
                    jnp.concatenate([lines[3 * ch + g][:, j].reshape(128, LANES) for g in range(GROUPS)], axis=0)
                    for ch in range(GROUPS)
                ],
                axis=1,
            )
            low = full.astype(BF16)
            left = dot(coul, low).astype(BF16)
            bare = dot(left, coul)
            screened.append(bare + dot(left, bare.astype(BF16)))
        for ch in range(GROUPS):
            for g in range(GROUPS):
                both = [
                    s[128 * g : 128 * g + 128, LANES * ch : LANES * ch + LANES].reshape(16, 1, 8, LANES) for s in screened
                ]
                chain[3 * ch + g, :, rows, :] = jnp.concatenate(both, axis=1).reshape(16, 16, LANES).astype(BF16)
        return carry

    order = [3 * ch + g for g in range(GROUPS) for ch in range(GROUPS)]
    for wp in range(NT // 2):
        pair(wp, 0)
    for n in order:
        send(2, n)

    last = []
    def weigh_part(n):
        ch = n // GROUPS

        def weigh(i, carry):
            rows = pl.ds(pl.multiple_of(32 * i, 32), 32)
            here = pl.ds(pl.multiple_of(32 * lax.rem(i, 2), 32), 32)
            screens = [screen[n, 2 * q + i // 2, here, :].astype(F32) for q in range(NK)]
            for c in range(NK):
                total = None
                for q in range(NK):
                    term = aux_s[n, source_ref[q, c], rows, :] * screens[q]
                    total = term if total is None else total + term
                sum_s[c, rows, LANES * ch : LANES * ch + LANES] = total.astype(BF16)
            return carry

        lax.fori_loop(0, 4, weigh, 0)

    def halve(g):
        for s in range(NK):
            c = lax.bitwise_xor(pb, s)
            product = dot(sum_s[c], colloc_s[c]).reshape(2, NT, 8, 256)
            half_s[g, c] = jnp.stack([product[0], product[1]], axis=1).reshape(128, 256).astype(BF16)
            if s:
                pltpu.make_async_remote_copy(
                    src_ref=half_s.at[g, c],
                    dst_ref=out_ref.at[g, pb],
                    send_sem=last_send.at[g],
                    recv_sem=last_recv.at[g],
                    device_id=(c, ta),
                    device_id_type=MESH,
                ).start()
        own = pltpu.make_async_copy(half_s.at[g, pb], out_ref.at[g, pb], last_own.at[g])
        own.start()
        last.append(own)

    behind = 6
    for at in range(PARTS + behind):
        if at < PARTS:
            receive(2, order[at])
            transform(late_wide, back, stamps, order[at])
            send(3, order[at])
        if at >= behind:
            receive(3, order[at - behind])
            weigh_part(order[at - behind])
            if (at - behind) % GROUPS == GROUPS - 1:
                halve((at - behind) // GROUPS)
    for g in range(GROUPS):
        last[g].wait()
        part = out_ref.at[g, pl.ds(0, NK - 1)]
        pltpu.make_async_copy(part, part, last_recv.at[g]).wait()
        part = half_s.at[g, pl.ds(0, NK - 1)]
        pltpu.make_async_copy(part, part, last_send.at[g]).wait()
    for stage in range(4):
        for n in range(PARTS):
            sent(stage, n)


def step(kplus, green, colloc, to_freq, to_time, coulomb):
    block = (PARTS, 16, 64, LANES)
    vmem = pl.BlockSpec(memory_space=pltpu.VMEM)
    smem = pl.BlockSpec(memory_space=pltpu.SMEM)
    hbm = pl.BlockSpec(memory_space=pl.ANY)
    dma = pltpu.SemaphoreType.DMA
    return pl.pallas_call(
        step_kernel,
        in_specs=[smem, hbm, hbm, vmem, vmem, vmem],
        out_specs=hbm,
        out_shape=jax.ShapeDtypeStruct((GROUPS, NK, 128, 256), BF16),
        scratch_shapes=[
            pltpu.VMEM((NK, NT, 256, 256), BF16),
            pltpu.VMEM((NK, 384, 256), BF16),
            pltpu.VMEM((NK, 384, 256), BF16),
            pltpu.VMEM((NK, 384, 256), BF16),
            pltpu.VMEM((PARTS, NK, 128, LANES), F32),
            pltpu.VMEM((GROUPS, NK, 128, LANES), F32),
        ]
        + [pltpu.VMEM(block, BF16)] * 8
        + [
            pltpu.VMEM((1024, 1024), BF16),
            pltpu.VMEM((1024, 1024), BF16),
            pltpu.VMEM((NK, 128, 384), BF16),
            pltpu.VMEM((GROUPS, NK, 128, 256), BF16),
            pltpu.SMEM((NK, NK), jnp.int32),
            dma((NK + 1,)),
            dma((4, PARTS)),
            dma((4, PARTS)),
            dma((4, PARTS)),
            dma((GROUPS,)),
            dma((GROUPS,)),
            dma((GROUPS,)),
        ],
        compiler_params=pltpu.CompilerParams(collective_id=0, has_side_effects=True, vmem_limit_bytes=56 * MIB),
        name="step",
    )(kplus, green, colloc, to_freq, to_time, coulomb)


def sigma_kernel(place_ref, half_ref, colloc_ref, out_ref):
    for t in range(out_ref.shape[1]):
        out_ref[0, t] = dot(colloc_ref[0], half_ref[:, :, t].reshape(384, 256), ((0,), (0,))) * (-1.0 / NK)


def sigma(half, colloc, place):
    size = 4
    return pl.pallas_call(
        sigma_kernel,
        grid_spec=pltpu.PrefetchScalarGridSpec(
            num_scalar_prefetch=1,
            grid=(NT // size,),
            in_specs=[
                pl.BlockSpec((GROUPS, NK, size, 16, 256), lambda i, place: (0, 0, i, 0, 0)),
                pl.BlockSpec((1, 384, 256), lambda i, place: (place[0], 0, 0)),
            ],
            out_specs=pl.BlockSpec((1, size, 256, 256), lambda i, place: (0, i, 0, 0)),
        ),
        out_shape=jax.ShapeDtypeStruct((1, NT, 256, 256), F32),
        compiler_params=pltpu.CompilerParams(vmem_limit_bytes=56 * MIB),
        name="sigma",
    )(place, half.reshape(GROUPS, NK, NT, 16, 256), colloc)


def local(green, colloc, kplus, to_freq, to_time, coulomb):
    half = step(kplus, green, colloc, to_freq, to_time, coulomb)
    return sigma(half, colloc, lax.axis_index("pb").astype(jnp.int32).reshape(1))


def solution(mesh):
    in_specs = (P(None, "ta", None, None), P(), P(), P(), P(), P())
    out_specs = P("pb", "ta", None, None)
    return jax.shard_map(local, mesh=mesh, in_specs=in_specs, out_specs=out_specs, check_vma=False)
```

```python
import jax
import jax.numpy as jnp
from jax import lax
from jax.experimental import pallas as pl
from jax.experimental.pallas import tpu as pltpu
from jax.sharding import PartitionSpec as P

MESH = pl.DeviceIdType.MESH
F32, BF16 = jnp.float32, jnp.bfloat16
NK = 8
NT = 8
GROUPS = 3
PARTS = GROUPS * GROUPS
LANES = 128
MIB = 1 << 20


def dot(a, b, dims=((1,), (0,))):
    return lax.dot_general(a, b, (dims, ((), ())), preferred_element_type=F32)


def spread(table, wide_ref):
    row = lax.broadcasted_iota(jnp.int32, (1024, 128), 0) // 8
    pick = (row == lax.broadcasted_iota(jnp.int32, (1024, 128), 1)).astype(BF16)
    across = dot(table, pick, ((1,), (1,))).astype(BF16)
    for part in range(4):
        full = dot(pick[256 * part : 256 * part + 256], across)
        same = lax.broadcasted_iota(jnp.int32, (256, 1024), 0) % 8 == lax.broadcasted_iota(jnp.int32, (256, 1024), 1) % 8
        wide_ref[256 * part : 256 * part + 256, :] = jnp.where(same, full, 0.0).astype(BF16)


def transform(wide_ref, src, dst, n):
    x = src[n].reshape(1024, LANES)
    for part in range(4):
        y = dot(wide_ref[256 * part : 256 * part + 256, :], x)
        dst[n, 4 * part : 4 * part + 4] = y.astype(BF16).reshape(4, 64, LANES)


def step_kernel(
    kplus_ref, green_ref, colloc_ref, freq_ref, time_ref, coul_ref, out_ref,
    green_s, colloc_s, rows_s, left_s, right_s, aux_s, mirror_s, polar, times, freqs, whole, chain, back, stamps, screen, wide,
    late_wide, sum_s, half_s, source_ref, load_sem, send_sem, recv_sem, own_sem, last_send, last_recv, last_own,
):
    pb, ta = lax.axis_index("pb"), lax.axis_index("ta")
    z_hi, x = pb >> 2, pb & 3
    z_lo, y, core = ta >> 3, (ta >> 1) & 3, ta & 1
    own_q = y + 4 * (z_lo ^ z_hi)
    own_block = 2 * pb + core

    def load(k):
        return pltpu.make_async_copy(green_ref.at[k], green_s.at[k], load_sem.at[k])

    def load_rows(g):
        rows = pl.ds(pl.multiple_of(128 * g + 16 * pb, 16), 16)
        return pltpu.make_async_copy(colloc_ref.at[:, rows, :], rows_s.at[:, g], load_sem.at[NK + 1 + g])

    load_colloc = pltpu.make_async_copy(colloc_ref, colloc_s, load_sem.at[NK])
    for g in range(GROUPS):
        load_rows(g).start()
    for k in range(NK):
        load(k).start()
    load_colloc.start()

    way = 1 - 2 * core

    def split(s, at, z):
        ring = ((s >> 1) & 1) | ((s >> 3) << 1)
        return (at + way * ring) & 3, z ^ (s & 1), core ^ ((s >> 2) & 1)

    def line(s):
        other_y, other_z, other_core = split(s, y, z_lo)
        return ((other_z << 3) | (other_y << 1) | other_core), (pb, (other_z << 3) | (other_y << 1) | other_core)

    def line_transfer(s):
        other, device = line(s)
        return other ^ (z_hi << 3), device

    def plane(s):
        other_x, other_z, other_core = split(s, x, z_hi)
        other = (other_z << 2) | other_x
        return (other << 1) | other_core, (other, ((z_lo ^ z_hi ^ other_z) << 3) | (y << 1) | other_core)

    def last_partner(s):
        return ((z_hi ^ (s & 1)) << 2) | ((x + way * (s >> 1)) & 3)

    stages = (
        (polar, times, ta, line_transfer),
        (freqs, whole, own_block, plane),
        (chain, back, own_block, plane),
        (stamps, screen, 2 * own_q + core, line),
    )

    def send(stage, n):
        src, dst, there, partner = stages[stage]

        def go(s, carry):
            slot, device = partner(s)
            pltpu.make_async_remote_copy(
                src_ref=src.at[n, slot],
                dst_ref=dst.at[n, there],
                send_sem=send_sem.at[stage, n],
                recv_sem=recv_sem.at[stage, n],
                device_id=device,
                device_id_type=MESH,
            ).start()
            return carry

        lax.fori_loop(1, 16, go, 0, unroll=True)
        pltpu.make_async_copy(src.at[n, partner(0)[0]], dst.at[n, there], own_sem.at[stage, n]).start()

    def receive(stage, n):
        src, dst, there, partner = stages[stage]
        part = dst.at[n, pl.ds(0, 15)]
        pltpu.make_async_copy(part, part, recv_sem.at[stage, n]).wait()
        pltpu.make_async_copy(src.at[n, partner(0)[0]], dst.at[n, there], own_sem.at[stage, n]).wait()

    def sent(stage, n):
        part = stages[stage][0].at[n, pl.ds(0, 15)]
        pltpu.make_async_copy(part, part, send_sem.at[stage, n]).wait()

    barrier = pltpu.get_barrier_semaphore()

    def greet(s, carry):
        pl.semaphore_signal(barrier, inc=1, device_id=line(s)[1], device_id_type=MESH)
        pl.semaphore_signal(barrier, inc=1, device_id=plane(s)[1], device_id_type=MESH)
        return carry

    def greet_last(s, carry):
        pl.semaphore_signal(barrier, inc=1, device_id=(pb ^ s, ta), device_id_type=MESH)
        return carry

    lax.fori_loop(1, 16, greet, 0)
    lax.fori_loop(1, NK, greet_last, 0)

    for g in range(GROUPS):
        load_rows(g).wait()

    def project(k, carry):
        load(k).wait()
        rows = rows_s[k].reshape(48, 256)
        left = [dot(rows, green_s[k, t]).reshape(6, 1, 8, 256) for t in range(NT)]
        right = [dot(rows, green_s[k, t ^ 1], ((1,), (1,))).reshape(6, 1, 8, 256) for t in range(NT)]
        left_s[k] = jnp.concatenate(left, axis=1).reshape(384, 256).astype(BF16)
        right_s[k] = jnp.concatenate(right, axis=1).reshape(384, 256).astype(BF16)
        return carry

    lax.fori_loop(0, NK, project, 0)
    load_colloc.wait()
    pl.semaphore_wait(barrier, 30 + NK - 1)

    for ch in range(GROUPS):

        def widen(k, carry):
            columns = colloc_s[k, LANES * ch : LANES * ch + LANES, :]
            aux = dot(left_s[k], columns, ((1,), (1,)))
            mirror = dot(right_s[k], columns, ((1,), (1,)))
            for g in range(GROUPS):
                aux_s[3 * ch + g, k] = aux[128 * g : 128 * g + 128]
                mirror_s[g, k] = mirror[128 * g : 128 * g + 128]
            return carry

        lax.fori_loop(0, NK, widen, 0, unroll=True)
        for g in range(GROUPS):
            n = 3 * ch + g

            def polarize(i, carry):
                rows = pl.ds(pl.multiple_of(32 * i, 32), 32)
                mirrors = [mirror_s[g, k, rows, :] for k in range(NK)]
                for q in range(NK):
                    total = None
                    for k in range(NK):
                        term = aux_s[n, kplus_ref[q, k], rows, :] * mirrors[k]
                        total = term if total is None else total + term
                    polar[n, 2 * q + i // 2, pl.ds(pl.multiple_of(32 * lax.rem(i, 2), 32), 32), :] = (
                        total * (-1.0 / NK)
                    ).astype(BF16)
                return carry

            lax.fori_loop(0, 4, polarize, 0)
            send(0, n)
        if ch == 0:
            spread(freq_ref[...], wide)

    def find(i, carry):
        q, c = i // NK, lax.rem(i, NK)
        found = jnp.int32(0)
        for k in range(NK):
            found = jnp.where(kplus_ref[q, k] == c, k, found)
        source_ref[q, c] = found
        return carry

    for n in range(PARTS):
        receive(0, n)
        transform(wide, times, freqs, n)
        send(1, n)
        if n == PARTS // 2:
            spread(time_ref[...], late_wide)
            lax.fori_loop(0, NK * NK, find, 0)
    for n in range(PARTS):
        receive(1, n)

    def pair(wp, carry):
        coul = coul_ref[...]
        rows = pl.ds(pl.multiple_of(16 * wp, 16), 16)
        lines = [whole[n, :, rows, :].astype(F32).reshape(16, 2, 8, LANES) for n in range(PARTS)]
        full = []
        for j in range(2):
            matrix = jnp.concatenate(
                [
                    jnp.concatenate([lines[3 * ch + g][:, j].reshape(128, LANES) for g in range(GROUPS)], axis=0)
                    for ch in range(GROUPS)
                ],
                axis=1,
            )
            full.append(matrix.astype(BF16))
        lefts = dot(coul, jnp.concatenate(full, axis=1)).astype(BF16)
        screened = []
        for j in range(2):
            left = lefts[:, 384 * j : 384 * j + 384]
            bare = dot(left, coul)
            screened.append(bare + dot(left, bare.astype(BF16)))
        for ch in range(GROUPS):
            for g in range(GROUPS):
                both = [
                    s[128 * g : 128 * g + 128, LANES * ch : LANES * ch + LANES].reshape(16, 1, 8, LANES) for s in screened
                ]
                chain[3 * ch + g, :, rows, :] = jnp.concatenate(both, axis=1).reshape(16, 16, LANES).astype(BF16)
        return carry

    order = [3 * ch + g for g in range(GROUPS) for ch in range(GROUPS)]
    for wp in range(NT // 2):
        pair(wp, 0)
    for n in order:
        send(2, n)

    last = []
    def weigh_part(n):
        ch = n // GROUPS

        def weigh(i, carry):
            rows = pl.ds(pl.multiple_of(32 * i, 32), 32)
            here = pl.ds(pl.multiple_of(32 * lax.rem(i, 2), 32), 32)
            screens = [screen[n, 2 * q + i // 2, here, :].astype(F32) for q in range(NK)]
            for c in range(NK):
                total = None
                for q in range(NK):
                    term = aux_s[n, source_ref[q, c], rows, :] * screens[q]
                    total = term if total is None else total + term
                sum_s[c, rows, LANES * ch : LANES * ch + LANES] = total.astype(BF16)
            return carry

        lax.fori_loop(0, 4, weigh, 0)

    def halve(g):
        for s in range(NK):
            c = last_partner(s)
            product = dot(sum_s[c], colloc_s[c]).reshape(2, NT, 8, 256)
            half_s[g, c] = jnp.stack([product[0], product[1]], axis=1).reshape(128, 256).astype(BF16)
            if s:
                pltpu.make_async_remote_copy(
                    src_ref=half_s.at[g, c],
                    dst_ref=out_ref.at[g, pb],
                    send_sem=last_send.at[g],
                    recv_sem=last_recv.at[g],
                    device_id=(c, ta),
                    device_id_type=MESH,
                ).start()
        own = pltpu.make_async_copy(half_s.at[g, pb], out_ref.at[g, pb], last_own.at[g])
        own.start()
        last.append(own)

    behind = 6
    for at in range(PARTS + behind):
        if at < PARTS:
            receive(2, order[at])
            transform(late_wide, back, stamps, order[at])
            send(3, order[at])
        if at >= behind:
            receive(3, order[at - behind])
            weigh_part(order[at - behind])
            if (at - behind) % GROUPS == GROUPS - 1:
                halve((at - behind) // GROUPS)
    for g in range(GROUPS):
        last[g].wait()
        part = out_ref.at[g, pl.ds(0, NK - 1)]
        pltpu.make_async_copy(part, part, last_recv.at[g]).wait()
        part = half_s.at[g, pl.ds(0, NK - 1)]
        pltpu.make_async_copy(part, part, last_send.at[g]).wait()
    for stage in range(4):
        for n in range(PARTS):
            sent(stage, n)


def step(kplus, green, colloc, to_freq, to_time, coulomb):
    block = (PARTS, 16, 64, LANES)
    vmem = pl.BlockSpec(memory_space=pltpu.VMEM)
    smem = pl.BlockSpec(memory_space=pltpu.SMEM)
    hbm = pl.BlockSpec(memory_space=pl.ANY)
    dma = pltpu.SemaphoreType.DMA
    return pl.pallas_call(
        step_kernel,
        in_specs=[smem, hbm, hbm, vmem, vmem, vmem],
        out_specs=hbm,
        out_shape=jax.ShapeDtypeStruct((GROUPS, NK, 128, 256), BF16),
        scratch_shapes=[
            pltpu.VMEM((NK, NT, 256, 256), BF16),
            pltpu.VMEM((NK, 384, 256), BF16),
            pltpu.VMEM((NK, GROUPS, 16, 256), BF16),
            pltpu.VMEM((NK, 384, 256), BF16),
            pltpu.VMEM((NK, 384, 256), BF16),
            pltpu.VMEM((PARTS, NK, 128, LANES), F32),
            pltpu.VMEM((GROUPS, NK, 128, LANES), F32),
        ]
        + [pltpu.VMEM(block, BF16)] * 8
        + [
            pltpu.VMEM((1024, 1024), BF16),
            pltpu.VMEM((1024, 1024), BF16),
            pltpu.VMEM((NK, 128, 384), BF16),
            pltpu.VMEM((GROUPS, NK, 128, 256), BF16),
            pltpu.SMEM((NK, NK), jnp.int32),
            dma((NK + 1 + GROUPS,)),
            dma((4, PARTS)),
            dma((4, PARTS)),
            dma((4, PARTS)),
            dma((GROUPS,)),
            dma((GROUPS,)),
            dma((GROUPS,)),
        ],
        compiler_params=pltpu.CompilerParams(collective_id=0, has_side_effects=True, vmem_limit_bytes=56 * MIB),
        name="step",
    )(kplus, green, colloc, to_freq, to_time, coulomb)


def sigma_kernel(place_ref, half_ref, colloc_ref, out_ref):
    for t in range(out_ref.shape[1]):
        out_ref[0, t] = dot(colloc_ref[0], half_ref[:, :, t].reshape(384, 256), ((0,), (0,))) * (-1.0 / NK)


def sigma(half, colloc, place):
    size = 4
    return pl.pallas_call(
        sigma_kernel,
        grid_spec=pltpu.PrefetchScalarGridSpec(
            num_scalar_prefetch=1,
            grid=(NT // size,),
            in_specs=[
                pl.BlockSpec((GROUPS, NK, size, 16, 256), lambda i, place: (0, 0, i, 0, 0)),
                pl.BlockSpec((1, 384, 256), lambda i, place: (place[0], 0, 0)),
            ],
            out_specs=pl.BlockSpec((1, size, 256, 256), lambda i, place: (0, i, 0, 0)),
        ),
        out_shape=jax.ShapeDtypeStruct((1, NT, 256, 256), F32),
        compiler_params=pltpu.CompilerParams(vmem_limit_bytes=56 * MIB),
        name="sigma",
    )(place, half.reshape(GROUPS, NK, NT, 16, 256), colloc)


def local(green, colloc, kplus, to_freq, to_time, coulomb):
    half = step(kplus, green, colloc, to_freq, to_time, coulomb)
    return sigma(half, colloc, lax.axis_index("pb").astype(jnp.int32).reshape(1))


def solution(mesh):
    in_specs = (P(None, "ta", None, None), P(), P(), P(), P(), P())
    out_specs = P("pb", "ta", None, None)
    return jax.shard_map(local, mesh=mesh, in_specs=in_specs, out_specs=out_specs, check_vma=False)
```

```python
import jax
import jax.numpy as jnp
from jax import lax
from jax.experimental import pallas as pl
from jax.experimental.pallas import tpu as pltpu
from jax.sharding import PartitionSpec as P

MESH = pl.DeviceIdType.MESH
F32, BF16 = jnp.float32, jnp.bfloat16
NK = 8
NT = 8
GROUPS = 3
PARTS = GROUPS * GROUPS
LANES = 128
MIB = 1 << 20


def dot(a, b, dims=((1,), (0,))):
    return lax.dot_general(a, b, (dims, ((), ())), preferred_element_type=F32)


def spread(table, wide_ref):
    row = lax.broadcasted_iota(jnp.int32, (1024, 128), 0) // 8
    pick = (row == lax.broadcasted_iota(jnp.int32, (1024, 128), 1)).astype(BF16)
    across = dot(table, pick, ((1,), (1,))).astype(BF16)
    for part in range(4):
        full = dot(pick[256 * part : 256 * part + 256], across)
        same = lax.broadcasted_iota(jnp.int32, (256, 1024), 0) % 8 == lax.broadcasted_iota(jnp.int32, (256, 1024), 1) % 8
        wide_ref[256 * part : 256 * part + 256, :] = jnp.where(same, full, 0.0).astype(BF16)


def transform(wide_ref, src, dst, n):
    x = src[n].reshape(1024, LANES)
    for part in range(4):
        y = dot(wide_ref[256 * part : 256 * part + 256, :], x)
        dst[n, 4 * part : 4 * part + 4] = y.astype(BF16).reshape(4, 64, LANES)


def step_kernel(
    kplus_ref, green_ref, colloc_ref, freq_ref, time_ref, coul_ref, out_ref,
    green_s, colloc_s, rows_s, left_s, right_s, aux_s, mirror_s, polar, times, freqs, whole, chain, back, stamps, screen, wide,
    late_wide, sum_s, half_s, source_ref, load_sem, send_sem, recv_sem, own_sem, last_send, last_recv, last_own,
):
    pb, ta = lax.axis_index("pb"), lax.axis_index("ta")
    z_hi, x = pb >> 2, pb & 3
    z_lo, y, core = ta >> 3, (ta >> 1) & 3, ta & 1
    own_q = y + 4 * (z_lo ^ z_hi)
    own_block = 2 * pb + core

    def load(k):
        return pltpu.make_async_copy(green_ref.at[k], green_s.at[k], load_sem.at[k])

    def load_rows(g):
        rows = pl.ds(pl.multiple_of(128 * g + 16 * pb, 16), 16)
        return pltpu.make_async_copy(colloc_ref.at[:, rows, :], rows_s.at[:, g], load_sem.at[NK + 1 + g])

    load_colloc = pltpu.make_async_copy(colloc_ref, colloc_s, load_sem.at[NK])
    for g in range(GROUPS):
        load_rows(g).start()
    for k in range(NK):
        load(k).start()
    load_colloc.start()

    way = 1 - 2 * core

    def split(s, at, z):
        ring = ((s >> 1) & 1) | ((s >> 3) << 1)
        return (at + way * ring) & 3, z ^ (s & 1), core ^ ((s >> 2) & 1)

    def line(s):
        other_y, other_z, other_core = split(s, y, z_lo)
        return ((other_z << 3) | (other_y << 1) | other_core), (pb, (other_z << 3) | (other_y << 1) | other_core)

    def line_transfer(s):
        other, device = line(s)
        return other ^ (z_hi << 3), device

    def plane(s):
        other_x, other_z, other_core = split(s, x, z_hi)
        other = (other_z << 2) | other_x
        return (other << 1) | other_core, (other, ((z_lo ^ z_hi ^ other_z) << 3) | (y << 1) | other_core)

    def last_partner(s):
        return ((z_hi ^ (s & 1)) << 2) | ((x + way * (s >> 1)) & 3)

    stages = (
        (polar, times, ta, line_transfer),
        (freqs, whole, own_block, plane),
        (chain, back, own_block, plane),
        (stamps, screen, 2 * own_q + core, line),
    )

    def send(stage, n):
        src, dst, there, partner = stages[stage]

        def go(s, carry):
            slot, device = partner(s)
            pltpu.make_async_remote_copy(
                src_ref=src.at[n, slot],
                dst_ref=dst.at[n, there],
                send_sem=send_sem.at[stage, n],
                recv_sem=recv_sem.at[stage, n],
                device_id=device,
                device_id_type=MESH,
            ).start()
            return carry

        lax.fori_loop(1, 16, go, 0, unroll=True)
        pltpu.make_async_copy(src.at[n, partner(0)[0]], dst.at[n, there], own_sem.at[stage, n]).start()

    def receive(stage, n):
        src, dst, there, partner = stages[stage]
        part = dst.at[n, pl.ds(0, 15)]
        pltpu.make_async_copy(part, part, recv_sem.at[stage, n]).wait()
        pltpu.make_async_copy(src.at[n, partner(0)[0]], dst.at[n, there], own_sem.at[stage, n]).wait()

    def sent(stage, n):
        part = stages[stage][0].at[n, pl.ds(0, 15)]
        pltpu.make_async_copy(part, part, send_sem.at[stage, n]).wait()

    barrier = pltpu.get_barrier_semaphore()

    def greet(s, carry):
        pl.semaphore_signal(barrier, inc=1, device_id=line(s)[1], device_id_type=MESH)
        pl.semaphore_signal(barrier, inc=1, device_id=plane(s)[1], device_id_type=MESH)
        return carry

    def greet_last(s, carry):
        pl.semaphore_signal(barrier, inc=1, device_id=(pb ^ s, ta), device_id_type=MESH)
        return carry

    lax.fori_loop(1, 16, greet, 0)
    lax.fori_loop(1, NK, greet_last, 0)

    for g in range(GROUPS):
        load_rows(g).wait()

    def project(k, carry):
        load(k).wait()
        rows = rows_s[k].reshape(48, 256)
        left = [dot(rows, green_s[k, t]).reshape(6, 1, 8, 256) for t in range(NT)]
        right = [dot(rows, green_s[k, t ^ 1], ((1,), (1,))).reshape(6, 1, 8, 256) for t in range(NT)]
        left_s[k] = jnp.concatenate(left, axis=1).reshape(384, 256).astype(BF16)
        right_s[k] = jnp.concatenate(right, axis=1).reshape(384, 256).astype(BF16)
        return carry

    lax.fori_loop(0, NK, project, 0)
    load_colloc.wait()
    pl.semaphore_wait(barrier, 30 + NK - 1)

    for ch in range(GROUPS):

        def widen(k, carry):
            columns = colloc_s[k, LANES * ch : LANES * ch + LANES, :]
            aux = dot(left_s[k], columns, ((1,), (1,)))
            mirror = dot(right_s[k], columns, ((1,), (1,)))
            for g in range(GROUPS):
                aux_s[3 * ch + g, k] = aux[128 * g : 128 * g + 128]
                mirror_s[g, k] = mirror[128 * g : 128 * g + 128]
            return carry

        lax.fori_loop(0, NK, widen, 0, unroll=True)
        for g in range(GROUPS):
            n = 3 * ch + g

            def polarize(i, carry):
                rows = pl.ds(pl.multiple_of(32 * i, 32), 32)
                mirrors = [mirror_s[g, k, rows, :] for k in range(NK)]
                for q in range(NK):
                    total = None
                    for k in range(NK):
                        term = aux_s[n, kplus_ref[q, k], rows, :] * mirrors[k]
                        total = term if total is None else total + term
                    polar[n, 2 * q + i // 2, pl.ds(pl.multiple_of(32 * lax.rem(i, 2), 32), 32), :] = (
                        total * (-1.0 / NK)
                    ).astype(BF16)
                return carry

            lax.fori_loop(0, 4, polarize, 0)
            send(0, n)
        if ch == 0:
            spread(freq_ref[...], wide)

    def find(i, carry):
        q, c = i // NK, lax.rem(i, NK)
        found = jnp.int32(0)
        for k in range(NK):
            found = jnp.where(kplus_ref[q, k] == c, k, found)
        source_ref[q, c] = found
        return carry

    for n in range(PARTS):
        receive(0, n)
        transform(wide, times, freqs, n)
        send(1, n)
        if n == PARTS // 2:
            spread(time_ref[...], late_wide)
            lax.fori_loop(0, NK * NK, find, 0)
    for n in range(PARTS):
        receive(1, n)

    def pair(wp, carry):
        coul = coul_ref[...]
        rows = pl.ds(pl.multiple_of(16 * wp, 16), 16)
        lines = [whole[n, :, rows, :].astype(F32).reshape(16, 2, 8, LANES) for n in range(PARTS)]
        full = []
        for j in range(2):
            matrix = jnp.concatenate(
                [
                    jnp.concatenate([lines[3 * ch + g][:, j].reshape(128, LANES) for g in range(GROUPS)], axis=0)
                    for ch in range(GROUPS)
                ],
                axis=1,
            )
            full.append(matrix.astype(BF16))
        lefts = dot(coul, jnp.concatenate(full, axis=1)).astype(BF16)
        screened = []
        for j in range(2):
            left = lefts[:, 384 * j : 384 * j + 384]
            bare = dot(left, coul)
            screened.append(bare + dot(left, bare.astype(BF16)))
        for ch in range(GROUPS):
            for g in range(GROUPS):
                both = [
                    s[128 * g : 128 * g + 128, LANES * ch : LANES * ch + LANES].reshape(16, 1, 8, LANES) for s in screened
                ]
                chain[3 * ch + g, :, rows, :] = jnp.concatenate(both, axis=1).reshape(16, 16, LANES).astype(BF16)
        return carry

    order = [3 * ch + g for g in range(GROUPS) for ch in range(GROUPS)]
    for wp in range(NT // 2):
        pair(wp, 0)
    for n in order:
        send(2, n)

    last = []
    def weigh_part(n):
        ch = n // GROUPS

        def weigh(i, carry):
            rows = pl.ds(pl.multiple_of(32 * i, 32), 32)
            here = pl.ds(pl.multiple_of(32 * lax.rem(i, 2), 32), 32)
            screens = [screen[n, 2 * q + i // 2, here, :].astype(F32) for q in range(NK)]
            for c in range(NK):
                total = None
                for q in range(NK):
                    term = aux_s[n, source_ref[q, c], rows, :] * screens[q]
                    total = term if total is None else total + term
                sum_s[c, rows, LANES * ch : LANES * ch + LANES] = total.astype(BF16)
            return carry

        lax.fori_loop(0, 4, weigh, 0)

    def halve(g):
        for s in range(NK):
            c = last_partner(s)
            product = dot(sum_s[c], colloc_s[c]).reshape(2, NT, 8, 256)
            half_s[g, c] = jnp.stack([product[0], product[1]], axis=1).reshape(128, 256).astype(BF16)
            if s:
                pltpu.make_async_remote_copy(
                    src_ref=half_s.at[g, c],
                    dst_ref=out_ref.at[g, pb],
                    send_sem=last_send.at[g],
                    recv_sem=last_recv.at[g],
                    device_id=(c, ta),
                    device_id_type=MESH,
                ).start()
        own = pltpu.make_async_copy(half_s.at[g, pb], out_ref.at[g, pb], last_own.at[g])
        own.start()
        last.append(own)

    behind = 7
    for at in range(PARTS + behind):
        if at < PARTS:
            receive(2, order[at])
            transform(late_wide, back, stamps, order[at])
            send(3, order[at])
        if at >= behind:
            receive(3, order[at - behind])
            weigh_part(order[at - behind])
            if (at - behind) % GROUPS == GROUPS - 1:
                halve((at - behind) // GROUPS)
    for g in range(GROUPS):
        last[g].wait()
        part = out_ref.at[g, pl.ds(0, NK - 1)]
        pltpu.make_async_copy(part, part, last_recv.at[g]).wait()
        part = half_s.at[g, pl.ds(0, NK - 1)]
        pltpu.make_async_copy(part, part, last_send.at[g]).wait()
    for stage in range(4):
        for n in range(PARTS):
            sent(stage, n)


def step(kplus, green, colloc, to_freq, to_time, coulomb):
    block = (PARTS, 16, 64, LANES)
    vmem = pl.BlockSpec(memory_space=pltpu.VMEM)
    smem = pl.BlockSpec(memory_space=pltpu.SMEM)
    hbm = pl.BlockSpec(memory_space=pl.ANY)
    dma = pltpu.SemaphoreType.DMA
    return pl.pallas_call(
        step_kernel,
        in_specs=[smem, hbm, hbm, vmem, vmem, vmem],
        out_specs=hbm,
        out_shape=jax.ShapeDtypeStruct((GROUPS, NK, 128, 256), BF16),
        scratch_shapes=[
            pltpu.VMEM((NK, NT, 256, 256), BF16),
            pltpu.VMEM((NK, 384, 256), BF16),
            pltpu.VMEM((NK, GROUPS, 16, 256), BF16),
            pltpu.VMEM((NK, 384, 256), BF16),
            pltpu.VMEM((NK, 384, 256), BF16),
            pltpu.VMEM((PARTS, NK, 128, LANES), F32),
            pltpu.VMEM((GROUPS, NK, 128, LANES), F32),
        ]
        + [pltpu.VMEM(block, BF16)] * 8
        + [
            pltpu.VMEM((1024, 1024), BF16),
            pltpu.VMEM((1024, 1024), BF16),
            pltpu.VMEM((NK, 128, 384), BF16),
            pltpu.VMEM((GROUPS, NK, 128, 256), BF16),
            pltpu.SMEM((NK, NK), jnp.int32),
            dma((NK + 1 + GROUPS,)),
            dma((4, PARTS)),
            dma((4, PARTS)),
            dma((4, PARTS)),
            dma((GROUPS,)),
            dma((GROUPS,)),
            dma((GROUPS,)),
        ],
        compiler_params=pltpu.CompilerParams(collective_id=0, has_side_effects=True, vmem_limit_bytes=56 * MIB),
        name="step",
    )(kplus, green, colloc, to_freq, to_time, coulomb)


def sigma_kernel(place_ref, half_ref, colloc_ref, out_ref):
    for t in range(out_ref.shape[1]):
        out_ref[0, t] = dot(colloc_ref[0], half_ref[:, :, t].reshape(384, 256), ((0,), (0,))) * (-1.0 / NK)


def sigma(half, colloc, place):
    size = 4
    return pl.pallas_call(
        sigma_kernel,
        grid_spec=pltpu.PrefetchScalarGridSpec(
            num_scalar_prefetch=1,
            grid=(NT // size,),
            in_specs=[
                pl.BlockSpec((GROUPS, NK, size, 16, 256), lambda i, place: (0, 0, i, 0, 0)),
                pl.BlockSpec((1, 384, 256), lambda i, place: (place[0], 0, 0)),
            ],
            out_specs=pl.BlockSpec((1, size, 256, 256), lambda i, place: (0, i, 0, 0)),
        ),
        out_shape=jax.ShapeDtypeStruct((1, NT, 256, 256), F32),
        compiler_params=pltpu.CompilerParams(vmem_limit_bytes=56 * MIB),
        name="sigma",
    )(place, half.reshape(GROUPS, NK, NT, 16, 256), colloc)


def local(green, colloc, kplus, to_freq, to_time, coulomb):
    half = step(kplus, green, colloc, to_freq, to_time, coulomb)
    return sigma(half, colloc, lax.axis_index("pb").astype(jnp.int32).reshape(1))


def solution(mesh):
    in_specs = (P(None, "ta", None, None), P(), P(), P(), P(), P())
    out_specs = P("pb", "ta", None, None)
    return jax.shard_map(local, mesh=mesh, in_specs=in_specs, out_specs=out_specs, check_vma=False)
```

```python
import jax
import jax.numpy as jnp
from jax import lax
from jax.experimental import pallas as pl
from jax.experimental.pallas import tpu as pltpu
from jax.sharding import PartitionSpec as P

MESH = pl.DeviceIdType.MESH
F32, BF16 = jnp.float32, jnp.bfloat16
NK = 8
NT = 8
GROUPS = 3
PARTS = GROUPS * GROUPS
LANES = 128
MIB = 1 << 20


def dot(a, b, dims=((1,), (0,))):
    return lax.dot_general(a, b, (dims, ((), ())), preferred_element_type=F32)


def spread(table, wide_ref):
    row = lax.broadcasted_iota(jnp.int32, (1024, 128), 0) // 8
    pick = (row == lax.broadcasted_iota(jnp.int32, (1024, 128), 1)).astype(BF16)
    across = dot(table, pick, ((1,), (1,))).astype(BF16)
    for part in range(4):
        full = dot(pick[256 * part : 256 * part + 256], across)
        same = lax.broadcasted_iota(jnp.int32, (256, 1024), 0) % 8 == lax.broadcasted_iota(jnp.int32, (256, 1024), 1) % 8
        wide_ref[256 * part : 256 * part + 256, :] = jnp.where(same, full, 0.0).astype(BF16)


def transform(wide_ref, src, dst, n):
    x = src[n].reshape(1024, LANES)
    for part in range(4):
        y = dot(wide_ref[256 * part : 256 * part + 256, :], x)
        dst[n, 4 * part : 4 * part + 4] = y.astype(BF16).reshape(4, 64, LANES)


def step_kernel(
    kplus_ref, green_ref, colloc_ref, freq_ref, time_ref, coul_ref, out_ref,
    green_s, colloc_s, rows_s, left_s, right_s, aux_s, mirror_s, polar, times, freqs, whole, chain, back, stamps, screen, wide,
    late_wide, sum_s, early_s, half_s, source_ref, load_sem, send_sem, recv_sem, own_sem, last_send, last_recv, last_own,
):
    pb, ta = lax.axis_index("pb"), lax.axis_index("ta")
    z_hi, x = pb >> 2, pb & 3
    z_lo, y, core = ta >> 3, (ta >> 1) & 3, ta & 1
    own_q = y + 4 * (z_lo ^ z_hi)
    own_block = 2 * pb + core

    def load(k):
        return pltpu.make_async_copy(green_ref.at[k], green_s.at[k], load_sem.at[k])

    def load_rows(g):
        rows = pl.ds(pl.multiple_of(128 * g + 16 * pb, 16), 16)
        return pltpu.make_async_copy(colloc_ref.at[:, rows, :], rows_s.at[:, g], load_sem.at[NK + 1 + g])

    load_colloc = pltpu.make_async_copy(colloc_ref, colloc_s, load_sem.at[NK])
    for g in range(GROUPS):
        load_rows(g).start()
    for k in range(NK):
        load(k).start()
    load_colloc.start()

    way = 1 - 2 * core

    def split(s, at, z):
        ring = ((s >> 1) & 1) | ((s >> 3) << 1)
        return (at + way * ring) & 3, z ^ (s & 1), core ^ ((s >> 2) & 1)

    def line(s):
        other_y, other_z, other_core = split(s, y, z_lo)
        return ((other_z << 3) | (other_y << 1) | other_core), (pb, (other_z << 3) | (other_y << 1) | other_core)

    def line_transfer(s):
        other, device = line(s)
        return other ^ (z_hi << 3), device

    def plane(s):
        other_x, other_z, other_core = split(s, x, z_hi)
        other = (other_z << 2) | other_x
        return (other << 1) | other_core, (other, ((z_lo ^ z_hi ^ other_z) << 3) | (y << 1) | other_core)

    def last_partner(s):
        return ((z_hi ^ (s & 1)) << 2) | ((x + way * (s >> 1)) & 3)

    stages = (
        (polar, times, ta, line_transfer),
        (freqs, whole, own_block, plane),
        (chain, back, own_block, plane),
        (stamps, screen, 2 * own_q + core, line),
    )

    def send(stage, n):
        src, dst, there, partner = stages[stage]

        def go(s, carry):
            slot, device = partner(s)
            pltpu.make_async_remote_copy(
                src_ref=src.at[n, slot],
                dst_ref=dst.at[n, there],
                send_sem=send_sem.at[stage, n],
                recv_sem=recv_sem.at[stage, n],
                device_id=device,
                device_id_type=MESH,
            ).start()
            return carry

        lax.fori_loop(1, 16, go, 0, unroll=True)
        pltpu.make_async_copy(src.at[n, partner(0)[0]], dst.at[n, there], own_sem.at[stage, n]).start()

    def receive(stage, n):
        src, dst, there, partner = stages[stage]
        part = dst.at[n, pl.ds(0, 15)]
        pltpu.make_async_copy(part, part, recv_sem.at[stage, n]).wait()
        pltpu.make_async_copy(src.at[n, partner(0)[0]], dst.at[n, there], own_sem.at[stage, n]).wait()

    def sent(stage, n):
        part = stages[stage][0].at[n, pl.ds(0, 15)]
        pltpu.make_async_copy(part, part, send_sem.at[stage, n]).wait()

    barrier = pltpu.get_barrier_semaphore()

    def greet(s, carry):
        pl.semaphore_signal(barrier, inc=1, device_id=line(s)[1], device_id_type=MESH)
        pl.semaphore_signal(barrier, inc=1, device_id=plane(s)[1], device_id_type=MESH)
        return carry

    def greet_last(s, carry):
        pl.semaphore_signal(barrier, inc=1, device_id=(pb ^ s, ta), device_id_type=MESH)
        return carry

    lax.fori_loop(1, 16, greet, 0)
    lax.fori_loop(1, NK, greet_last, 0)

    for g in range(GROUPS):
        load_rows(g).wait()

    def project(k, carry):
        load(k).wait()
        rows = rows_s[k].reshape(48, 256)
        left = [dot(rows, green_s[k, t]).reshape(6, 1, 8, 256) for t in range(NT)]
        right = [dot(rows, green_s[k, t ^ 1], ((1,), (1,))).reshape(6, 1, 8, 256) for t in range(NT)]
        left_s[k] = jnp.concatenate(left, axis=1).reshape(384, 256).astype(BF16)
        right_s[k] = jnp.concatenate(right, axis=1).reshape(384, 256).astype(BF16)
        return carry

    lax.fori_loop(0, NK, project, 0)
    load_colloc.wait()
    pl.semaphore_wait(barrier, 30 + NK - 1)

    for ch in range(GROUPS):

        def widen(k, carry):
            columns = colloc_s[k, LANES * ch : LANES * ch + LANES, :]
            aux = dot(left_s[k], columns, ((1,), (1,)))
            mirror = dot(right_s[k], columns, ((1,), (1,)))
            for g in range(GROUPS):
                aux_s[3 * ch + g, k] = aux[128 * g : 128 * g + 128]
                mirror_s[g, k] = mirror[128 * g : 128 * g + 128]
            return carry

        lax.fori_loop(0, NK, widen, 0, unroll=True)
        for g in range(GROUPS):
            n = 3 * ch + g

            def polarize(i, carry):
                rows = pl.ds(pl.multiple_of(32 * i, 32), 32)
                mirrors = [mirror_s[g, k, rows, :] for k in range(NK)]
                for q in range(NK):
                    total = None
                    for k in range(NK):
                        term = aux_s[n, kplus_ref[q, k], rows, :] * mirrors[k]
                        total = term if total is None else total + term
                    polar[n, 2 * q + i // 2, pl.ds(pl.multiple_of(32 * lax.rem(i, 2), 32), 32), :] = (
                        total * (-1.0 / NK)
                    ).astype(BF16)
                return carry

            lax.fori_loop(0, 4, polarize, 0)
            send(0, n)
        if ch == 0:
            spread(freq_ref[...], wide)

    def find(i, carry):
        q, c = i // NK, lax.rem(i, NK)
        found = jnp.int32(0)
        for k in range(NK):
            found = jnp.where(kplus_ref[q, k] == c, k, found)
        source_ref[q, c] = found
        return carry

    for n in range(PARTS):
        receive(0, n)
        transform(wide, times, freqs, n)
        send(1, n)
        if n == PARTS // 2:
            spread(time_ref[...], late_wide)
            lax.fori_loop(0, NK * NK, find, 0)
    for n in range(PARTS):
        receive(1, n)

    def pair(wp, carry):
        coul = coul_ref[...]
        rows = pl.ds(pl.multiple_of(16 * wp, 16), 16)
        lines = [whole[n, :, rows, :].astype(F32).reshape(16, 2, 8, LANES) for n in range(PARTS)]
        full = []
        for j in range(2):
            matrix = jnp.concatenate(
                [
                    jnp.concatenate([lines[3 * ch + g][:, j].reshape(128, LANES) for g in range(GROUPS)], axis=0)
                    for ch in range(GROUPS)
                ],
                axis=1,
            )
            full.append(matrix.astype(BF16))
        lefts = dot(coul, jnp.concatenate(full, axis=1)).astype(BF16)
        screened = []
        for j in range(2):
            left = lefts[:, 384 * j : 384 * j + 384]
            bare = dot(left, coul)
            screened.append(bare + dot(left, bare.astype(BF16)))
        for ch in range(GROUPS):
            for g in range(GROUPS):
                both = [
                    s[128 * g : 128 * g + 128, LANES * ch : LANES * ch + LANES].reshape(16, 1, 8, LANES) for s in screened
                ]
                chain[3 * ch + g, :, rows, :] = jnp.concatenate(both, axis=1).reshape(16, 16, LANES).astype(BF16)
        return carry

    order = [3 * ch + g for g in range(GROUPS) for ch in range(GROUPS)]
    for wp in range(NT // 2):
        pair(wp, 0)
    for n in order:
        send(2, n)

    last = []
    def weigh_part(n):
        ch = n // GROUPS

        def weigh(i, carry):
            rows = pl.ds(pl.multiple_of(32 * i, 32), 32)
            here = pl.ds(pl.multiple_of(32 * lax.rem(i, 2), 32), 32)
            screens = [screen[n, 2 * q + i // 2, here, :].astype(F32) for q in range(NK)]
            for c in range(NK):
                total = None
                for q in range(NK):
                    term = aux_s[n, source_ref[q, c], rows, :] * screens[q]
                    total = term if total is None else total + term
                sum_s[c, rows, LANES * ch : LANES * ch + LANES] = total.astype(BF16)
            return carry

        lax.fori_loop(0, 4, weigh, 0)

    def halve(g):
        for s in range(NK):
            c = last_partner(s)
            product = early_s[c] + dot(sum_s[c, :, 256:384], colloc_s[c, 256:384, :])
            product = product.reshape(2, NT, 8, 256)
            half_s[g, c] = jnp.stack([product[0], product[1]], axis=1).reshape(128, 256).astype(BF16)
            if s:
                pltpu.make_async_remote_copy(
                    src_ref=half_s.at[g, c],
                    dst_ref=out_ref.at[g, pb],
                    send_sem=last_send.at[g],
                    recv_sem=last_recv.at[g],
                    device_id=(c, ta),
                    device_id_type=MESH,
                ).start()
        own = pltpu.make_async_copy(half_s.at[g, pb], out_ref.at[g, pb], last_own.at[g])
        own.start()
        last.append(own)

    behind = 7
    for at in range(PARTS + behind):
        if at < PARTS:
            receive(2, order[at])
            transform(late_wide, back, stamps, order[at])
            send(3, order[at])
        if at >= behind:
            receive(3, order[at - behind])
            weigh_part(order[at - behind])
            if (at - behind) % GROUPS == GROUPS - 2:
                for c in range(NK):
                    early_s[c] = dot(sum_s[c, :, :256], colloc_s[c, :256, :])
            if (at - behind) % GROUPS == GROUPS - 1:
                halve((at - behind) // GROUPS)
    for g in range(GROUPS):
        last[g].wait()
        part = out_ref.at[g, pl.ds(0, NK - 1)]
        pltpu.make_async_copy(part, part, last_recv.at[g]).wait()
        part = half_s.at[g, pl.ds(0, NK - 1)]
        pltpu.make_async_copy(part, part, last_send.at[g]).wait()
    for stage in range(4):
        for n in range(PARTS):
            sent(stage, n)


def step(kplus, green, colloc, to_freq, to_time, coulomb):
    block = (PARTS, 16, 64, LANES)
    vmem = pl.BlockSpec(memory_space=pltpu.VMEM)
    smem = pl.BlockSpec(memory_space=pltpu.SMEM)
    hbm = pl.BlockSpec(memory_space=pl.ANY)
    dma = pltpu.SemaphoreType.DMA
    return pl.pallas_call(
        step_kernel,
        in_specs=[smem, hbm, hbm, vmem, vmem, vmem],
        out_specs=hbm,
        out_shape=jax.ShapeDtypeStruct((GROUPS, NK, 128, 256), BF16),
        scratch_shapes=[
            pltpu.VMEM((NK, NT, 256, 256), BF16),
            pltpu.VMEM((NK, 384, 256), BF16),
            pltpu.VMEM((NK, GROUPS, 16, 256), BF16),
            pltpu.VMEM((NK, 384, 256), BF16),
            pltpu.VMEM((NK, 384, 256), BF16),
            pltpu.VMEM((PARTS, NK, 128, LANES), F32),
            pltpu.VMEM((GROUPS, NK, 128, LANES), F32),
        ]
        + [pltpu.VMEM(block, BF16)] * 8
        + [
            pltpu.VMEM((1024, 1024), BF16),
            pltpu.VMEM((1024, 1024), BF16),
            pltpu.VMEM((NK, 128, 384), BF16),
            pltpu.VMEM((NK, 128, 256), F32),
            pltpu.VMEM((GROUPS, NK, 128, 256), BF16),
            pltpu.SMEM((NK, NK), jnp.int32),
            dma((NK + 1 + GROUPS,)),
            dma((4, PARTS)),
            dma((4, PARTS)),
            dma((4, PARTS)),
            dma((GROUPS,)),
            dma((GROUPS,)),
            dma((GROUPS,)),
        ],
        compiler_params=pltpu.CompilerParams(collective_id=0, has_side_effects=True, vmem_limit_bytes=56 * MIB),
        name="step",
    )(kplus, green, colloc, to_freq, to_time, coulomb)


def sigma_kernel(place_ref, half_ref, colloc_ref, out_ref):
    for t in range(out_ref.shape[1]):
        out_ref[0, t] = dot(colloc_ref[0], half_ref[:, :, t].reshape(384, 256), ((0,), (0,))) * (-1.0 / NK)


def sigma(half, colloc, place):
    size = 4
    return pl.pallas_call(
        sigma_kernel,
        grid_spec=pltpu.PrefetchScalarGridSpec(
            num_scalar_prefetch=1,
            grid=(NT // size,),
            in_specs=[
                pl.BlockSpec((GROUPS, NK, size, 16, 256), lambda i, place: (0, 0, i, 0, 0)),
                pl.BlockSpec((1, 384, 256), lambda i, place: (place[0], 0, 0)),
            ],
            out_specs=pl.BlockSpec((1, size, 256, 256), lambda i, place: (0, i, 0, 0)),
        ),
        out_shape=jax.ShapeDtypeStruct((1, NT, 256, 256), F32),
        compiler_params=pltpu.CompilerParams(vmem_limit_bytes=56 * MIB),
        name="sigma",
    )(place, half.reshape(GROUPS, NK, NT, 16, 256), colloc)


def local(green, colloc, kplus, to_freq, to_time, coulomb):
    half = step(kplus, green, colloc, to_freq, to_time, coulomb)
    return sigma(half, colloc, lax.axis_index("pb").astype(jnp.int32).reshape(1))


def solution(mesh):
    in_specs = (P(None, "ta", None, None), P(), P(), P(), P(), P())
    out_specs = P("pb", "ta", None, None)
    return jax.shard_map(local, mesh=mesh, in_specs=in_specs, out_specs=out_specs, check_vma=False)
```
